128 devices in a mesh: req: 4 (over y), wx: 8 (over x, core), wy: 4 (over z).
Axes of the slice: x: 4, y: 4, z: 4, core: 2. Of those that a mesh axis runs over, the one named last changes fastest.
Arguments:
- tokens: bfloat16 [2048, 8192], P('req', 'wy'), may hold values from -6 to 6
- w_in_x: bfloat16 [8192, 8192], P('wy', 'wx'), may hold values from -0.0625 to 0.0625
- w_in_z: bfloat16 [8192, 8192], P('wy', 'wx'), may hold values from -0.0625 to 0.0625
- conv_weight: float32 [4, 8192], P(None, ('wx', 'wy')), may hold values from -3 to 3
- conv_bias: float32 [8192], P(('wx', 'wy')), may hold values from -3 to 3
- w_xproj: bfloat16 [8192, 544], P(('wx', 'wy')), may hold values from -0.0625 to 0.0625
- w_dt: bfloat16 [512, 8192], P(None, ('wx', 'wy')), may hold values from -0.25 to 0.25
- dt_bias: float32 [8192], P(('wx', 'wy')), may hold values from -2 to 0.5
- a_rate: float32 [16, 8192], P(None, ('wx', 'wy')), may hold values from 0.25 to 8
- d_skip: float32 [8192], P(('wx', 'wy')), may hold values from 0.5 to 1.5
- w_out: bfloat16 [8192, 8192], P(('wx', 'wy')), may hold values from -0.0625 to 0.0625
- ssm_state: float32 [512, 16, 8192], P('req', None, ('wx', 'wy')), may hold values from -6 to 6
- conv_state: bfloat16 [512, 3, 8192], P('req', None, ('wx', 'wy')), may hold values from -6 to 6
- accepted: int32 [512], P('req'), may hold values from 0 to 4
- offsets: int32 [512], P('req'), may hold values from 0 to 2044, as said below
Outputs:
- mixed_out: bfloat16 [2048, 8192], P(('req', 'wx', 'wy'))
- new_ssm: float32 [512, 16, 8192], P('req', None, ('wx', 'wy'))
- new_conv: bfloat16 [512, 3, 8192], P('req', None, ('wx', 'wy'))
The draws below stay inside these ranges and needn't reach their ends.
Inputs may be any that keep to these rules, and one draw needn't show every extreme that they name: Request r owns packed rows offsets[r] to offsets[r] + 3; the requests of the b-th block of 128 requests fill exactly the b-th block of 512 rows, in some order.
All inputs are finite; a program needn't handle non-finite values.
Results may differ from the reference program's by a relative error of at most 0.008.
Values may be sent and summed in bfloat16 or wider, within the bound.
No kernel may reach another device: no remote copies, remote signals or barrier semaphores. Data moves between devices by JAX's collectives and lax.ppermute only.
A program may use at most 128 MiB of HBM per device.

```python
import math
import jax
import jax.numpy as jnp

D = 8192
E = 8192
RANK = 512
NST = 16
CONV = 4
DRAFT = 4
REQ_GRP = 128
TOK_GRP = 512
REQS = 512
TOKENS = 2048
N_REQ = 4


def draw_offsets(key, part):
    key = jax.random.fold_in(key, 7)
    group_keys = jax.random.split(key, N_REQ)
    orders = jax.vmap(lambda single: jax.random.permutation(single, REQ_GRP))(group_keys)
    starts = jnp.arange(N_REQ, dtype=jnp.int32)[:, None] * TOK_GRP
    return (starts + DRAFT * orders.astype(jnp.int32)).reshape(-1).astype(jnp.int32)


def place_ends(result, rng, least, top_value):
    extent = result.shape
    index_at = [jax.random.randint(jax.random.fold_in(rng, axis), (), 0, extent[axis]) for axis in range(len(extent))]
    result = result.at[tuple(index_at)].set(least)
    longest = extent.index(max(extent))
    index_at[longest] = (index_at[longest] + 1) % extent[longest]
    return result.at[tuple(index_at)].set(top_value)


def block_scale(stream_key, dims, shards, smallest, largest):
    def one(dim, shards_of):
        heights = jax.random.uniform(jax.random.fold_in(jax.random.fold_in(stream_key, 6), dim), (shards_of,), jnp.float32, smallest / len(shards), largest / len(shards))
        return jnp.repeat(jnp.exp(heights), dims[dim] // shards_of).reshape((-1,) + (1,) * (len(dims) - dim - 1))

    gain = one(*shards[0])
    for cut in shards[1:]:
        gain = gain * one(*cut)
    return gain


def centred(rng, dims, width, limit, cuts=(), kind=jnp.bfloat16):
    array = width * jax.random.normal(rng, dims, jnp.float32)
    if cuts:
        array = array * block_scale(rng, dims, cuts, -0.22, 0.18)
    return jnp.clip(array, -limit, limit).astype(kind)


def setup_inputs(seed: int = 0) -> dict:
    streams_of = jax.random.split(jax.random.key(seed), 16)
    tokens = centred(streams_of[0], (TOKENS, D), 1.0, 6.0, ((0, 4), (1, 4)))
    w_in_x = centred(streams_of[1], (D, E), D ** -0.5, 0.0625, ((0, 4), (1, 8)))
    w_in_z = centred(streams_of[2], (D, E), D ** -0.5, 0.0625, ((0, 4), (1, 8)))
    conv_weight = centred(streams_of[3], (CONV, E), CONV ** -0.5, 3.0, ((1, 32),), jnp.float32)
    conv_bias = centred(streams_of[4], (E,), 0.5, 3.0, ((0, 32),), jnp.float32)
    w_xproj = centred(streams_of[5], (E, RANK + 2 * NST), E ** -0.5, 0.0625, ((0, 32),))
    w_dt = centred(streams_of[6], (RANK, E), RANK ** -0.5, 0.25, ((1, 32),))
    dt_bias = jnp.clip(-2.0 + 2.5 * jax.random.uniform(streams_of[7], (E,), jnp.float32) ** block_scale(streams_of[7], (E,), ((0, 32),), -0.2, 0.2), -2.0, 0.5)
    a_rate = jnp.clip(jnp.exp(math.log(8.0) - 3.465736 * jax.random.uniform(streams_of[8], (NST, E), jnp.float32) ** block_scale(streams_of[8], (NST, E), ((1, 32),), -0.2, 0.2)), 0.25, 8.0)
    d_skip = jnp.clip(0.5 + 1.0 * jax.random.uniform(streams_of[9], (E,), jnp.float32) ** block_scale(streams_of[9], (E,), ((0, 32),), -0.2, 0.2), 0.5, 1.5)
    w_out = centred(streams_of[10], (E, D), E ** -0.5, 0.0625, ((0, 32),))
    ssm_state = centred(streams_of[11], (REQS, NST, E), 1.0, 6.0, ((0, 4), (2, 32)), jnp.float32)
    conv_state = centred(streams_of[12], (REQS, CONV - 1, E), 1.0, 6.0, ((0, 4), (2, 32)))
    accepted = place_ends(jax.random.randint(streams_of[13], (REQS,), 0, DRAFT + 1), jax.random.fold_in(streams_of[13], 1), 0, DRAFT).astype(jnp.int32)
    offsets = draw_offsets(jax.random.fold_in(streams_of[15], 71), 0)
    return dict(tokens=tokens, w_in_x=w_in_x, w_in_z=w_in_z, conv_weight=conv_weight, conv_bias=conv_bias, w_xproj=w_xproj, w_dt=w_dt, dt_bias=dt_bias, a_rate=a_rate, d_skip=d_skip, w_out=w_out, ssm_state=ssm_state, conv_state=conv_state, accepted=accepted, offsets=offsets)


def verify_core(draft_x, draft_z, conv_weight, conv_bias, projected_fn, w_dt, dt_bias, a_rate, d_skip, ssm_state, conv_state, accepted):
    requests = draft_x.shape[0]
    drafts = draft_x.shape[1]
    taps = conv_weight.shape[0]
    chans = draft_x.shape[2]
    history = jnp.concatenate([conv_state, draft_x], axis=1)
    conv_sum = jnp.zeros((requests, drafts, chans), jnp.float32) + conv_bias[None, None, :]
    for tap in range(taps):
        conv_sum = conv_sum + history[:, tap:tap + drafts].astype(jnp.float32) * conv_weight[tap][None, None, :]
    conv_out = jax.nn.silu(conv_sum).astype(jnp.bfloat16)
    projected = projected_fn(conv_out.reshape(requests * drafts, chans))
    rank = w_dt.shape[0]
    nstate = a_rate.shape[0]
    dt_input = projected[:, :rank].astype(jnp.bfloat16)
    b_in = projected[:, rank:rank + nstate].reshape(requests, drafts, nstate)
    c_out = projected[:, rank + nstate:].reshape(requests, drafts, nstate)
    step_size = jax.nn.softplus(jnp.dot(dt_input, w_dt, preferred_element_type=jnp.float32) + dt_bias[None, :])
    step_size = step_size.reshape(requests, drafts, chans)
    gate_vals = jax.nn.silu(draft_z.astype(jnp.float32))
    state = ssm_state
    kept = ssm_state
    results = []
    for position in range(drafts):
        xvalue = conv_out[:, position].astype(jnp.float32)
        delta = step_size[:, position]
        decay = jnp.exp(-delta[:, None, :] * a_rate[None, :, :])
        state = decay * state + (delta * xvalue)[:, None, :] * b_in[:, position, :, None]
        kept = jnp.where((accepted == position + 1)[:, None, None], state, kept)
        readout = jnp.sum(c_out[:, position, :, None] * state, axis=1) + d_skip[None, :] * xvalue
        results.append(readout * gate_vals[:, position])
    scanned = jnp.stack(results, axis=1).astype(jnp.bfloat16)
    window = history[:, 0:taps - 1]
    for shift_by in range(1, drafts + 1):
        window = jnp.where((accepted == shift_by)[:, None, None], history[:, shift_by:shift_by + taps - 1], window)
    return scanned, kept, window


def reference(tokens, w_in_x, w_in_z, conv_weight, conv_bias, w_xproj, w_dt, dt_bias, a_rate, d_skip, w_out, ssm_state, conv_state, accepted, offsets):
    inner_x = jnp.dot(tokens, w_in_x, preferred_element_type=jnp.float32).astype(jnp.bfloat16)
    inner_z = jnp.dot(tokens, w_in_z, preferred_element_type=jnp.float32).astype(jnp.bfloat16)
    row_index = (offsets[:, None] + jnp.arange(DRAFT, dtype=jnp.int32)[None, :]).astype(jnp.int32)
    flat_index = row_index.reshape(-1)
    draft_x = jnp.take(inner_x, flat_index, axis=0).reshape(REQS, DRAFT, E)
    draft_z = jnp.take(inner_z, flat_index, axis=0).reshape(REQS, DRAFT, E)

    def project_all(flat_conv):
        return jnp.dot(flat_conv, w_xproj, preferred_element_type=jnp.float32)

    scanned, new_ssm, new_conv = verify_core(draft_x, draft_z, conv_weight, conv_bias, project_all, w_dt, dt_bias, a_rate, d_skip, ssm_state, conv_state, accepted)
    packed = jnp.zeros((TOKENS, E), jnp.bfloat16).at[flat_index].set(scanned.reshape(REQS * DRAFT, E))
    mixed_out = jnp.dot(packed, w_out, preferred_element_type=jnp.float32).astype(jnp.bfloat16)
    return (mixed_out, new_ssm, new_conv)
```

```python
import functools
import math

import jax
import jax.numpy as jnp
from jax import lax
from jax.experimental import pallas as pl
from jax.experimental.pallas import tpu as pltpu
from jax.sharding import PartitionSpec as P

DRAFT = 4
BF = jnp.bfloat16
F32 = jnp.float32
LOG2E = math.log2(math.e)


def params(megabytes=16):
    return pltpu.CompilerParams(vmem_limit_bytes=megabytes * 1024 * 1024)


def cost(flops, nbytes, transcendentals=0):
    return pl.CostEstimate(
        flops=int(flops), bytes_accessed=int(nbytes), transcendentals=int(transcendentals)
    )


def near(value):
    return pltpu.with_memory_space_constraint(value, pltpu.VMEM)


def far(value):
    return pltpu.with_memory_space_constraint(value, pltpu.HBM)


def dot(a, b):
    return jnp.dot(a, b, preferred_element_type=F32)


def dot_rows(a, b):
    return lax.dot_general(a, b, (((1,), (1,)), ((), ())), preferred_element_type=F32)


VM = pl.BlockSpec(memory_space=pltpu.VMEM)
ANY = pl.BlockSpec(memory_space=pl.ANY)
HBM = pl.BlockSpec(memory_space=pltpu.HBM)


def swap_core(value):
    return lax.ppermute(value, "core", [(0, 1), (1, 0)])


def swap_x(value, d):
    return lax.ppermute(value, "x", [(i, i ^ d) for i in range(4)])


def swap_z(value, d):
    return lax.ppermute(value, "wy", [(i, i ^ d) for i in range(4)])


def swap_by_core(value, *ways):
    def index(x, core, z):
        return (x * 2 + core) * 4 + z

    pairs = []
    for x in range(4):
        for core, (axis, d) in enumerate(ways):
            for z in range(4):
                there = (x ^ d, core, z) if axis == "x" else (x, core, z ^ d)
                pairs.append((index(x, core, z), index(*there)))
    return lax.ppermute(value, ("x", "core", "wy"), pairs)


CHUNKS = 4


def multiply(tok, w_ref, w_held, total, sems, tok_ref=None, tok_sems=None):
    depth = w_held.shape[0] // CHUNKS
    slices = [pl.ds(i * depth, depth) for i in range(CHUNKS)]
    copies = []
    for i, here in enumerate(slices):
        copies.append([pltpu.make_async_copy(w_ref.at[here], w_held.at[here], sems.at[i])])
        if tok_ref is not None:
            copies[i].append(
                pltpu.make_async_copy(tok_ref.at[:, here], tok.at[:, here], tok_sems.at[i])
            )
        for copy in copies[i]:
            copy.start()
    for i in range(CHUNKS):
        for copy in copies[i]:
            copy.wait()
        here = slice(i * depth, (i + 1) * depth)
        value = dot(tok[:, here], w_held[here])
        if i == 0:
            total[...] = value
        else:
            total[...] += value


def block_of(total, d):
    chans = total.shape[1] // 4
    return pl.ds(pl.multiple_of((lax.axis_index("wy") ^ d) * chans, chans), chans)


def hand_out(total, send, kept):
    first = 1 + 2 * lax.axis_index("core")
    for out, blocks in ((send, (first, 2)), (kept, (first ^ 2, 0))):
        for i, d in enumerate(blocks):
            out[i] = total[:, block_of(total, d)].astype(out.dtype)


def project_x_kernel(tok_ref, w_ref, send_1, send_2, send_3, kept, tok, w_held, total, sems, tok_sems):
    multiply(tok, w_ref, w_held, total, sems, tok_ref, tok_sems)
    first = 1 + 2 * lax.axis_index("core")
    for out, d in ((send_1, first), (send_2, first ^ 2), (send_3, 2), (kept, 0)):
        out[...] = total[:, block_of(total, d)].astype(out.dtype)


def project_z_kernel(tok, w_ref, after_ref, send, kept, w_held, total, sems):
    del after_ref
    multiply(tok, w_ref, w_held, total, sems)
    hand_out(total, send, kept)


def branch_shapes(rows, weights):
    shape = (2, rows, weights.shape[1] // 4)
    return [pltpu.VMEM(shape, BF), pltpu.VMEM(shape, F32)]


def project_x(tokens, weights):
    rows, depth = tokens.shape
    shape = (rows, weights.shape[1] // 4)
    return pl.pallas_call(
        project_x_kernel,
        in_specs=[HBM, HBM],
        out_specs=[VM] * 5,
        out_shape=[pltpu.VMEM(shape, BF)] * 3
        + [pltpu.VMEM(shape, F32), pltpu.VMEM(tokens.shape, BF)],
        scratch_shapes=[
            pltpu.VMEM(weights.shape, BF),
            pltpu.VMEM((rows, weights.shape[1]), F32),
            pltpu.SemaphoreType.DMA((CHUNKS,)),
            pltpu.SemaphoreType.DMA((CHUNKS,)),
        ],
        compiler_params=params(),
        cost_estimate=cost(2 * rows * depth * weights.shape[1], 12e6),
    )(far(tokens), far(weights))


def project_z(tok, weights, after):
    rows, depth = tok.shape
    return pl.pallas_call(
        project_z_kernel,
        in_specs=[VM, HBM, ANY],
        out_specs=[VM] * 2,
        out_shape=branch_shapes(rows, weights),
        scratch_shapes=[
            pltpu.VMEM(weights.shape, BF),
            pltpu.VMEM((rows, weights.shape[1]), F32),
            pltpu.SemaphoreType.DMA((CHUNKS,)),
        ],
        compiler_params=params(),
        cost_estimate=cost(2 * rows * depth * weights.shape[1], 12e6),
    )(near(tok), far(weights), after)


def first_over_z(send):
    return swap_by_core(send, ("z", 1), ("z", 3))


def second_over_z(kept, got):
    return swap_by_core((kept[0] + got[1].astype(F32)).astype(BF), ("z", 3), ("z", 1))


def exchange_x(x_parts, z_parts):
    send_1, send_2, send_3, kept = x_parts
    got = (
        swap_by_core(send_1, ("z", 1), ("z", 3)),
        swap_by_core(send_2, ("z", 3), ("z", 1)),
        swap_z(send_3, 2),
    )
    *got, z_send, z_kept = lax.optimization_barrier((*got, *z_parts))
    return (kept, *got), [z_send, z_kept]


def assemble(kept_ref, got_ref, last_ref):
    return (kept_ref[1] + got_ref[0].astype(F32) + last_ref[...].astype(F32)).astype(BF)


def column(row_ref):
    size = row_ref.shape[1]
    across = lax.broadcasted_iota(jnp.int32, (size, size), 1)
    down = lax.broadcasted_iota(jnp.int32, (size, size), 0)
    spread = jnp.broadcast_to(row_ref[...].astype(F32), (size, size))
    return jnp.sum(jnp.where(across == down, spread, 0.0), axis=1, keepdims=True).astype(jnp.int32)


def draft_rows(value, first_row, position):
    spots = lax.broadcasted_iota(jnp.int32, (first_row.shape[0], value.shape[0]), 1)
    chosen = jnp.where(spots == first_row + position, 1.0, 0.0).astype(BF)
    return dot(chosen, value)


def conv_kernel(
    off_ref, kept_ref, got_1, got_2, got_3, hist_ref, cw_ref, cb_ref, wx_ref, send_ref, own_ref,
    draft_ref, conv_ref, both
):
    value = add_up(kept_ref[...], [got[...] for got in (got_1, got_2, got_3)]).astype(BF)
    first_row = column(off_ref) % value.shape[0]
    history = [hist_ref[k].astype(F32) for k in range(3)]
    for j in range(DRAFT):
        row = draft_rows(value, first_row, j)
        draft_ref[j] = row.astype(BF)
        history.append(row)
    rank = wx_ref.shape[0] - 32
    narrow = []
    for j in range(DRAFT):
        total = cb_ref[...] + history[j] * cw_ref[0:1]
        for k in range(1, 4):
            total = total + history[j + k] * cw_ref[k : k + 1]
        conv = (total / (1.0 + jnp.exp(-total))).astype(BF)
        conv_ref[j] = conv.astype(F32)
        both[:, j * rank : (j + 1) * rank] = dot_rows(conv, wx_ref[:rank])
        narrow.append(dot_rows(conv, wx_ref[rank:]))
    both[:, DRAFT * rank :] = jnp.concatenate(narrow, axis=1)
    core, me_x = lax.axis_index("core"), lax.axis_index("x")
    half = own_ref.shape[0]
    part = half // 4
    for index, out in ((1 - core, send_ref), (core, own_ref)):
        for d in range(4):
            start = pl.multiple_of(index * half + (me_x ^ d) * part, part)
            out[d * part : (d + 1) * part] = both[pl.ds(start, part)].astype(out.dtype)


def convolve(off_row, terms, hist, conv_weight, conv_bias, w_cols):
    requests = off_row.shape[1]
    chans = conv_weight.shape[1]
    wide = DRAFT * (w_cols.shape[0] - 32) + 128
    operands = (off_row, *terms, hist, conv_weight, conv_bias, w_cols)
    piece = (requests // 2, wide)
    return pl.pallas_call(
        conv_kernel,
        in_specs=[VM] * len(operands),
        out_specs=[VM] * 4,
        out_shape=[
            pltpu.VMEM(piece, BF),
            pltpu.VMEM(piece, F32),
            pltpu.VMEM((DRAFT, requests, chans), BF),
            pltpu.VMEM((DRAFT, requests, chans), F32),
        ],
        scratch_shapes=[pltpu.VMEM((requests, wide), F32)],
        compiler_params=params(),
        cost_estimate=cost(5e8, 4e6, 131072),
    )(*[near(v) for v in operands])


def gate_kernel(
    off_ref, acc_ref, kept_ref, got_ref, last_ref, hist_ref, draft_ref, gate_ref, window_ref
):
    value = assemble(kept_ref, got_ref, last_ref)
    first_row = column(off_ref) % value.shape[0]
    for j in range(DRAFT):
        row = draft_rows(value, first_row, j)
        gate_ref[j] = row / (1.0 + jnp.exp(-row))
    accepted = jnp.broadcast_to(column(acc_ref), draft_ref.shape[1:])
    history = [hist_ref[k].astype(F32) for k in range(3)]
    history += [draft_ref[j].astype(F32) for j in range(DRAFT)]
    for k in range(3):
        window = history[k]
        for shift in range(1, DRAFT + 1):
            window = jnp.where(accepted == shift, history[k + shift], window)
        window_ref[k] = window.astype(BF)


def gates(off_row, acc_row, terms, hist, draft):
    operands = (off_row, acc_row, *terms, hist, draft)
    return pl.pallas_call(
        gate_kernel,
        in_specs=[VM] * len(operands),
        out_specs=[VM] * 2,
        out_shape=[pltpu.VMEM(draft.shape, F32), jax.ShapeDtypeStruct(hist.shape, BF)],
        compiler_params=params(),
        cost_estimate=cost(2.7e8, 2e6, 131072),
    )(*[near(v) for v in operands])


def add_up(value, arrived):
    for one in arrived:
        value = value + one.astype(F32)
    return value


def sum_everywhere(send, own, z_parts, off_row, ssm_state):
    value = own + swap_core(send).astype(F32)
    part = value.shape[0] // 4
    got = [swap_x(value[d * part : (d + 1) * part].astype(BF), d) for d in (1, 3, 2)]
    z_send, z_kept = z_parts
    piece = add_up(value[:part], got)
    piece, z_got = lax.optimization_barrier((piece, first_over_z(z_send)))
    sent = piece.astype(BF)
    got = [swap_z(sent, d) for d in (1, 3, 2)]
    piece = add_up(piece, got).astype(BF)
    got = [swap_x(piece, d) for d in (1, 2, 3)]
    z_last = second_over_z(z_kept, z_got)
    *got, z_last, state, back = lax.optimization_barrier(
        (*got, z_last, *prepare(off_row, ssm_state, sent))
    )
    mine = jnp.concatenate([piece] + got, axis=0)
    return mine, swap_core(mine), (z_kept, z_got, z_last), state, back


PARTS = 4


def prepare_kernel(off_ref, state_ref, after_ref, turned_ref, back_ref, state_in, sems):
    del after_ref
    requests = state_ref.shape[0]
    rows = requests // PARTS
    loads = []
    for p in range(PARTS):
        here = pl.ds(p * rows, rows)
        loads.append(pltpu.make_async_copy(state_ref.at[here], state_in.at[here], sems.at[p]))
        loads[p].start()
    core, me_x, me_z = lax.axis_index("core"), lax.axis_index("x"), lax.axis_index("wy")
    places = back_ref.shape[2]
    place = lax.broadcasted_iota(jnp.int32, (places, requests), 0)
    token = (me_x ^ (place // 64)) * 128 + (me_z ^ ((place // 16) % 4)) * 16 + place % 16
    late = token - jnp.broadcast_to(off_ref[...] % (DRAFT * requests), (places, requests))
    for which, index in enumerate((core, 1 - core)):
        for j in range(DRAFT):
            back_ref[which, j] = jnp.where(late + index * 64 == j, 1.0, 0.0).astype(BF)
    for g in range(requests // 8):
        if (g * 8) % rows == 0:
            loads[g * 8 // rows].wait()
        here = slice(g * 8, g * 8 + 8)
        turned_ref[:, here] = jnp.swapaxes(state_in[here], 0, 1)


def prepare(off_row, state, after):
    requests, nstate, chans = state.shape
    return pl.pallas_call(
        prepare_kernel,
        in_specs=[VM, HBM, ANY],
        out_specs=[VM] * 2,
        out_shape=[
            pltpu.VMEM((nstate, requests, chans), F32),
            pltpu.VMEM((2, DRAFT, DRAFT * requests // 2, requests), BF),
        ],
        scratch_shapes=[pltpu.VMEM(state.shape, F32), pltpu.SemaphoreType.DMA((PARTS,))],
        compiler_params=params(),
        cost_estimate=cost(1e6, 4e6),
    )(near(off_row), far(state), after)


def scan_kernel(
    mine_ref, other_ref, wdt_ref, dtb_ref, a_ref, skip_ref, conv_ref, gate_ref, acc_ref, back_ref,
    state_ref, w_out_ref, w_other_ref, packed_ref, send_ref, kept_ref, w_near_ref, both, delta,
    result, rates, w_sems
):
    rank, chans = wdt_ref.shape
    nstate, requests, _ = state_ref.shape
    core, me_x = lax.axis_index("core"), lax.axis_index("x")
    moves = [
        pltpu.make_async_copy(ref, w_near_ref.at[i], w_sems.at[i])
        for i, ref in enumerate((w_out_ref, w_other_ref))
    ]
    for move in moves:
        move.start()
    half = mine_ref.shape[0]
    part = half // 4
    for index, ref in ((core, mine_ref), (1 - core, other_ref)):
        for d in range(4):
            start = pl.multiple_of(index * half + (me_x ^ d) * part, part)
            both[pl.ds(start, part)] = ref[d * part : (d + 1) * part]
    rates[...] = a_ref[...] * -LOG2E
    for j in range(DRAFT):
        pre = dot(both[:, j * rank : (j + 1) * rank], wdt_ref[...]) + dtb_ref[...]
        delta[j] = jnp.maximum(pre, 0.0) + jnp.log1p(jnp.exp(-jnp.abs(pre)))
    narrow = both[:, DRAFT * rank :].astype(F32)
    accepted_all = column(acc_ref)

    for g in range(requests // 8):
        here = slice(g * 8, g * 8 + 8)
        bc = narrow[here]
        accepted = jnp.broadcast_to(accepted_all[here], (8, chans))
        steps = [delta[j, here] for j in range(DRAFT)]
        convs = [conv_ref[j, here] for j in range(DRAFT)]
        drive = [steps[j] * convs[j] for j in range(DRAFT)]
        read = [skip_ref[...] * convs[j] for j in range(DRAFT)]
        for n in range(nstate):
            rate = rates[n : n + 1]
            state = state_ref[n, here]
            kept = state
            for j in range(DRAFT):
                b = bc[:, 32 * j + n : 32 * j + n + 1]
                c = bc[:, 32 * j + 16 + n : 32 * j + 16 + n + 1]
                state = jnp.exp2(steps[j] * rate) * state + drive[j] * b
                kept = jnp.where(accepted == j + 1, state, kept)
                read[j] = read[j] + c * state
            kept_ref[n, here] = kept
        for j in range(DRAFT):
            result[j, here] = read[j] * gate_ref[j, here]

    for which, out in enumerate((packed_ref, send_ref)):
        total = jnp.zeros(out.shape, F32)
        for j in range(DRAFT):
            total = total + dot(back_ref[which, j], result[j].astype(BF))
        out[...] = total.astype(BF)
    for move in moves:
        move.wait()


def scan(
    mine, other, w_dt, dt_bias, rates, skip, conv, gate, acc_row, back, state, w_out, w_other
):
    nstate, requests, chans = state.shape
    wide = DRAFT * w_dt.shape[0] + 128
    operands = (mine, other, w_dt, dt_bias, rates, skip, conv, gate, acc_row, back, state)
    packed = pltpu.VMEM((DRAFT * requests // 2, chans), BF)
    return pl.pallas_call(
        scan_kernel,
        in_specs=[VM] * len(operands) + [ANY, ANY],
        out_specs=[VM] * 4,
        out_shape=[
            packed,
            packed,
            pltpu.VMEM(state.shape, F32),
            pltpu.VMEM((2, *w_out.shape), BF),
        ],
        scratch_shapes=[
            pltpu.VMEM((requests, wide), BF),
            pltpu.VMEM((DRAFT, requests, chans), F32),
            pltpu.VMEM((DRAFT, requests, chans), F32),
            pltpu.VMEM((nstate, chans), F32),
            pltpu.SemaphoreType.DMA((2,)),
        ],
        compiler_params=params(),
        cost_estimate=cost(1e9, 6e6, 2.2e6),
    )(*[near(v) for v in operands], w_out, w_other)


STREAMS = (
    ("x", 1, 3, (1, 2), (0, 3)),
    ("x", 3, 1, (2, 3), (1, 0)),
    ("z", 1, 3, (1, 2), (0, 3)),
    ("z", 3, 1, (2, 3), (1, 0)),
)


def swap_of(axis):
    return swap_x if axis == "x" else swap_z


def stream_product(s, blocks, mine_ref, other_ref, w_ref):
    axis, part = STREAMS[s][0], w_ref.shape[2] // len(STREAMS)
    columns = slice(s * part, (s + 1) * part)
    value = 0.0
    for ref, w in ((mine_ref, 0), (other_ref, 1)):
        parts = [ref[i] if axis == "x" else ref[:, i] for i in blocks]
        rows = jnp.concatenate([p.reshape(64, p.shape[2]) for p in parts], axis=0)
        value = value + dot(rows, w_ref[w, :, columns])
    return value


def sent_kernel(s, mine_ref, other_ref, w_ref, out_ref):
    out_ref[...] = stream_product(s, STREAMS[s][3], mine_ref, other_ref, w_ref).astype(BF)


def project_sent(s, mine, other, w_near):
    part = w_near.shape[2] // len(STREAMS)
    return pl.pallas_call(
        functools.partial(sent_kernel, s),
        in_specs=[VM] * 3,
        out_specs=VM,
        out_shape=pltpu.VMEM((128, part), BF),
        compiler_params=params(),
        cost_estimate=cost(2 * 128 * 512 * part, 2e6),
    )(near(mine), near(other), near(w_near))


def held_kernel(kept_ref, mine_ref, other_ref, w_ref, *refs):
    outs, (state_ref, turned, sems) = refs[: len(STREAMS)], refs[len(STREAMS) :]
    rows = turned.shape[0] // PARTS
    stores = []
    for p in range(PARTS):
        for g in range(rows // 8):
            here = slice(p * rows + g * 8, p * rows + g * 8 + 8)
            turned[here] = jnp.swapaxes(kept_ref[:, here], 0, 1)
        here = pl.ds(p * rows, rows)
        stores.append(pltpu.make_async_copy(turned.at[here], state_ref.at[here], sems.at[p]))
        stores[p].start()
    for s, out in enumerate(outs):
        out[...] = stream_product(s, STREAMS[s][4], mine_ref, other_ref, w_ref)
    for store in stores:
        store.wait()


def project_held(kept, mine, other, w_near):
    nstate, requests, chans = kept.shape
    part = w_near.shape[2] // len(STREAMS)
    shape = (requests, nstate, chans)
    return pl.pallas_call(
        held_kernel,
        in_specs=[VM] * 4,
        out_specs=[VM] * 4 + [HBM],
        out_shape=[pltpu.VMEM((128, part), F32)] * 4 + [pltpu.HBM(shape, F32)],
        scratch_shapes=[pltpu.VMEM(shape, F32), pltpu.SemaphoreType.DMA((PARTS,))],
        compiler_params=params(),
        cost_estimate=cost(8 * 128 * 512 * part, 8e6),
    )(near(kept), near(mine), near(other), near(w_near))


def add_kernel(forward, held_ref, got_ref, own_ref, pass_ref):
    rows = own_ref.shape[0]
    own, send = (slice(0, rows), slice(rows, None))
    if not forward:
        own, send = send, own
    own_ref[...] = held_ref[own] + got_ref[own].astype(F32)
    pass_ref[...] = (held_ref[send] + got_ref[send].astype(F32)).astype(BF)


def add_arrived(s, held, got):
    shape = (held.shape[0] // 2, held.shape[1])
    return pl.pallas_call(
        functools.partial(add_kernel, STREAMS[s][1] == 1),
        in_specs=[VM] * 2,
        out_specs=[VM] * 2,
        out_shape=[pltpu.VMEM(shape, F32), pltpu.VMEM(shape, BF)],
        compiler_params=params(),
        cost_estimate=cost(held.size, 1e6),
    )(near(held), near(got))


def stage_kernel(own_a, got_a, own_b, got_b, keep_ref, *sends):
    size = keep_ref.shape[0]
    width = own_a.shape[1]
    for own, got, columns in (
        (own_a, got_a, slice(0, width)),
        (own_b, got_b, slice(width, None)),
    ):
        value = own[...] + got[...].astype(F32)
        keep_ref[:, columns] = value[:size]
        for d in range(1, 4):
            sends[d - 1][:, columns] = value[d * size : (d + 1) * size].astype(BF)


def next_stage(own_a, got_a, own_b, got_b):
    shape = (own_a.shape[0] // 4, 2 * own_a.shape[1])
    return pl.pallas_call(
        stage_kernel,
        in_specs=[VM] * 4,
        out_specs=[VM] * 4,
        out_shape=[pltpu.VMEM(shape, F32)] + [pltpu.VMEM(shape, BF)] * 3,
        compiler_params=params(),
        cost_estimate=cost(2 * own_a.size, 1e6),
    )(*[near(v) for v in (own_a, got_a, own_b, got_b)])


def last_kernel(*refs):
    left, right, out_ref = refs[:4], refs[4:8], refs[8]
    width = left[0].shape[1]
    for group, columns in ((left, slice(0, width)), (right, slice(width, None))):
        value = group[0][...]
        for one in group[1:]:
            value = value + one[...].astype(F32)
        out_ref[:, columns] = value.astype(BF)


def last_sum(left, right):
    rows, width = left[0].shape[0], left[0].shape[1] + right[0].shape[1]
    return pl.pallas_call(
        last_kernel,
        in_specs=[VM] * 8,
        out_specs=VM,
        out_shape=jax.ShapeDtypeStruct((rows, width), BF),
        compiler_params=params(),
        cost_estimate=cost(4 * rows * width, 1e6),
    )(*[near(v) for v in (*left, *right)])


def on_device(
    tokens,
    w_in_x,
    w_in_z,
    conv_weight,
    conv_bias,
    w_xproj,
    w_dt,
    dt_bias,
    a_rate,
    d_skip,
    w_out,
    ssm_state,
    conv_state,
    accepted,
    offsets,
):
    off_row, acc_row = offsets[None, :], accepted[None, :]
    hist = jnp.swapaxes(conv_state, 0, 1)

    w_other = swap_core(w_out)
    *x_parts, tok = project_x(tokens, w_in_x)
    z_parts = project_z(tok, w_in_z, x_parts[0])
    x_terms, z_parts = exchange_x(x_parts, z_parts)
    send, own, draft, conv = convolve(
        off_row, x_terms, hist, conv_weight, conv_bias[None, :], jnp.swapaxes(w_xproj, 0, 1)
    )
    z_parts[0], send = lax.optimization_barrier((z_parts[0], send))
    mine, other, z_terms, state, back = sum_everywhere(send, own, z_parts, off_row, ssm_state)
    gate, window = gates(off_row, acc_row, z_terms, hist, draft)
    packed, packed_send, kept, w_near = scan(
        mine,
        other,
        w_dt,
        dt_bias[None, :],
        a_rate,
        d_skip[None, :],
        conv,
        gate,
        acc_row,
        back,
        state,
        w_out,
        w_other,
    )
    new_conv = jnp.swapaxes(window, 0, 1)

    shape = (4, 4, 16, packed.shape[1])
    operands = (packed.reshape(shape), swap_core(packed_send).reshape(shape), w_near)
    got = []
    for s, (axis, one, *_) in enumerate(STREAMS):
        got.append(swap_of(axis)(project_sent(s, *operands), one))
    *helds, new_ssm = project_held(kept, *operands)
    results = []
    for s, (axis, _, two, *_) in enumerate(STREAMS):
        own_rows, passed = add_arrived(s, helds[s], got[s])
        results += [own_rows, swap_of(axis)(passed, two)]
    left, right = next_stage(*results[:4]), next_stage(*results[4:])
    left = (left[0], *[swap_z(left[d], d) for d in (2, 1, 3)])
    right = (right[0], *[swap_x(right[d], d) for d in (2, 1, 3)])
    mixed_out = last_sum(left, right)
    return (mixed_out, new_ssm, new_conv)


def solution(mesh):
    devices = mesh.devices.reshape(4, 4, 2, 4)
    fine = jax.sharding.Mesh(devices, ("req", "x", "core", "wy"))
    every = ("x", "core", "wy")
    wx = ("x", "core")
    placed = (
        P("req", "wy"),
        P("wy", wx),
        P("wy", wx),
        P(None, every),
        P(every),
        P(every, None),
        P(None, every),
        P(every),
        P(None, every),
        P(every),
        P(every, None),
        P("req", None, every),
        P("req", None, every),
        P("req"),
        P("req"),
    )
    return jax.shard_map(
        on_device,
        mesh=fine,
        in_specs=placed,
        out_specs=(
            P(("req", *every), None),
            P("req", None, every),
            P("req", None, every),
        ),
        check_vma=False,
    )
```
